32 devices in a mesh: dp: 8 (over z, y), tensor: 4 (over x, core).
Axes of the slice: x: 2, y: 2, z: 4, core: 2. Of those that a mesh axis runs over, the one named last changes fastest.
Arguments:
- tokens: float32 [16384, 768], P(('dp', 'tensor')), may hold values from -6 to 6
- seq_ids: int32 [16384], P('dp'), may hold values from 0 to 8, as said below
- gain_attn: float32 [768], replicated, may hold values from 0.5 to 1.5
- gain_mlp: float32 [768], replicated, may hold values from 0.5 to 1.5
- w_qkv: bfloat16 [3, 768, 768], P(None, None, 'tensor'), may hold values from -0.21875 to 0.21875
- w_out: bfloat16 [768, 768], P('tensor'), may hold values from -1.25 to 1.25
- w_gu: bfloat16 [2, 768, 1152], P(None, None, 'tensor'), may hold values from -0.21875 to 0.21875
- w_down: bfloat16 [1152, 768], P('tensor'), may hold values from -0.1875 to 0.1875
- cotangent: float32 [16384, 768], P(('dp', 'tensor')), may hold values from -6 to 6
Outputs:
- output: float32 [16384, 768], P(('dp', 'tensor'))
- input_grad: float32 [16384, 768], P(('dp', 'tensor'))
- gain_attn_grad: float32 [768], replicated
- gain_mlp_grad: float32 [768], replicated
- w_qkv_grad: float32 [3, 768, 768], P(None, None, 'tensor')
- w_out_grad: float32 [768, 768], P('tensor')
- w_gu_grad: float32 [2, 768, 1152], P(None, None, 'tensor')
- w_down_grad: float32 [1152, 768], P('tensor')
The draws below stay inside these ranges and needn't reach their ends.
Inputs may be any that keep to these rules, and one draw needn't show every extreme that they name: `seq_ids`: within each aligned block of 2048 tokens (those of one index of dp) the ids start at 0, never fall and rise by one at each new sequence; every sequence has 128 to 1024 tokens except a block's last one, which may be shorter; in every block some sequence has exactly 1024 tokens.
All inputs are finite; a program needn't handle non-finite values.
Results may differ from the reference program's by a relative error of at most 0.019.
Values may be sent and summed in bfloat16 or wider, within the bound.
A program may use at most 128 MiB of HBM per device.

```python
import jax
import jax.numpy as jnp
from jax import lax

D = 768
HEADS = 12
HEAD_DIM = 64
FF = 1152
TOK_DEV = 2048
MIN_LEN = 128
SEQ_LEN = 1024
TOKENS = 16384


def draw_seq_ids(key, part):
    key = jax.random.fold_in(key, 11)
    groups = TOKENS // TOK_DEV
    pieces = TOK_DEV // MIN_LEN + 1
    key_len, key_pick, key_dense = jax.random.split(key, 3)
    lengths = jax.random.randint(key_len, (groups, pieces), MIN_LEN, SEQ_LEN + 1)
    dense_group = jax.random.randint(key_dense, (), 0, groups)
    group_index = jnp.arange(groups, dtype=jnp.int32)[:, None]
    lengths = jnp.where(group_index == dense_group, MIN_LEN, lengths)
    chosen = jax.random.randint(key_pick, (groups, 1), 0, TOK_DEV // SEQ_LEN)
    slot_index = jnp.arange(pieces, dtype=jnp.int32)[None, :]
    lengths = jnp.where(slot_index == chosen, SEQ_LEN, lengths)
    bounds = jnp.cumsum(lengths, axis=1)
    places = jnp.arange(TOK_DEV, dtype=jnp.int32)
    seq_numbers = jnp.sum((bounds[:, None, :] <= places[None, :, None]).astype(jnp.int32), axis=2)
    return seq_numbers.reshape(TOKENS).astype(jnp.int32)


def levels(stream_key, shape, cuts, least, top_value):
    factor_of = 1.0
    for position, parts in cuts:
        steps = jax.random.uniform(jax.random.fold_in(jax.random.fold_in(stream_key, 6), position), (parts,), jnp.float32, least / len(cuts), top_value / len(cuts))
        factor_of = factor_of * jnp.repeat(jnp.exp(steps), shape[position] // parts).reshape((-1,) + (1,) * (len(shape) - 1 - position))
    return factor_of


def noise(rng, extent, scale, limit, shards=(), kind=jnp.bfloat16):
    result = jax.random.normal(rng, extent, jnp.float32) * scale
    if len(shards) > 0:
        result = levels(rng, extent, shards, -0.22, 0.18) * result
    return jnp.clip(result, min=-limit, max=limit).astype(kind)


def setup_inputs(seed: int = 0) -> dict:
    splits = jax.random.split(jax.random.key(seed), 10)
    return {
        "tokens": noise(splits[0], (TOKENS, D), 1.0, 6.0, ((0, 32),), jnp.float32),
        "seq_ids": draw_seq_ids(jax.random.fold_in(splits[9], 71), 0),
        "gain_attn": jnp.clip(1.0 + 0.1 * jax.random.normal(splits[2], (D,), jnp.float32), 0.5, 1.5),
        "gain_mlp": jnp.clip(1.0 + 0.1 * jax.random.normal(splits[3], (D,), jnp.float32), 0.5, 1.5),
        "w_qkv": noise(splits[4], (3, D, D), D ** -0.5, 0.21875, ((2, 4),)),
        "w_out": noise(splits[5], (D, D), (D // 32) ** -0.5, 1.25, ((0, 4),)),
        "w_gu": noise(splits[6], (2, D, FF), D ** -0.5, 0.21875, ((2, 4),)),
        "w_down": noise(splits[7], (FF, D), FF ** -0.5, 0.1875, ((0, 4),)),
        "cotangent": noise(splits[8], (TOKENS, D), 1.0, 6.0, ((0, 32),), jnp.float32),
    }


@jax.custom_vjp
def low(v):
    return lax.optimization_barrier(v.astype(jnp.bfloat16)).astype(jnp.float32)

@jax.custom_vjp
def low_back(v):
    return v

def low_keep(v):
    return (low(v), None)

def low_pass(kept, grad):
    return (grad,)

def back_keep(v):
    return (v, None)

def back_low(kept, grad):
    return (low(grad),)
low.defvjp(low_keep, low_pass)
low_back.defvjp(back_keep, back_low)
EPSILON = 1e-05
ROPE_BASE = 160000.0
HIGHEST = lax.Precision.HIGHEST

def layer_norm(values, gain_vec):
    center = values - lax.optimization_barrier(jnp.mean(values, axis=-1, keepdims=True))
    spread = lax.optimization_barrier(jnp.mean(center * center, axis=-1, keepdims=True))
    return center * lax.rsqrt(spread + EPSILON) * gain_vec

def positions_of(seq_rows):
    length = seq_rows.shape[-1]
    steps_all = jnp.arange(length, dtype=jnp.int32)
    before = jnp.concatenate([seq_rows[:, :1] - 1, seq_rows[:, :-1]], axis=1)
    change_marks = jnp.where(seq_rows != before, steps_all[None, :], 0).astype(jnp.int32)
    return (steps_all[None, :] - lax.cummax(change_marks, axis=1)).astype(jnp.float32)

def rotary_tables(places, width):
    half_width = width // 2
    frequency = ROPE_BASE ** (-(jnp.arange(half_width, dtype=jnp.float32) * 2.0) / width)
    angles = places[:, None] * frequency[None, :]
    cosine_tab = jnp.cos(angles)
    sine_tab = jnp.sin(angles)
    return (jnp.concatenate([cosine_tab, cosine_tab], axis=-1), jnp.concatenate([sine_tab, sine_tab], axis=-1))

def rotate(values, cosine_tab, sine_tab):
    half_width = values.shape[-1] // 2
    turned = jnp.concatenate([-values[..., half_width:], values[..., :half_width]], axis=-1)
    return values * cosine_tab[:, None, :] + turned * sine_tab[:, None, :]

def block_attend(query_blk, ids_blk, key_rows, value_rows, ids_rows):
    scores = jnp.einsum('qhd,khd->hqk', query_blk, key_rows, precision=HIGHEST) * HEAD_DIM ** (-0.5)
    scores = low_back(scores)
    same_seq = ids_blk[:, None] == ids_rows[None, :]
    scores = jnp.where(same_seq[None, :, :], scores, -1e+30)
    weights = low(jax.nn.softmax(scores, axis=-1))
    return jnp.einsum('hqk,khd->qhd', weights, value_rows, precision=HIGHEST)

def group_attend(group_item):
    query_rows, key_rows, value_rows, ids_rows = group_item
    length = query_rows.shape[0]
    block_rows = min(512, length)
    blocks = length // block_rows
    query_blocks = query_rows.reshape(blocks, block_rows, HEADS, HEAD_DIM)
    id_blocks = ids_rows.reshape(blocks, block_rows)

    def one_block(block_item):
        return block_attend(block_item[0], block_item[1], key_rows, value_rows, ids_rows)
    results = lax.map(jax.checkpoint(one_block), (query_blocks, id_blocks))
    return results.reshape(length, HEADS, HEAD_DIM)

def layer(inputs, gain_one, gain_two, qkv_weight, out_weight, gu_weight, down_weight, seq_ids):
    count_all = inputs.shape[0]
    groups = count_all // TOK_DEV
    normed = low(layer_norm(inputs, gain_one))
    projected = low_back(jnp.einsum('td,cde->cte', normed, qkv_weight, precision=HIGHEST))
    places = positions_of(seq_ids.reshape(groups, TOK_DEV)).reshape(count_all)
    cosine_tab, sine_tab = rotary_tables(places, HEAD_DIM)
    shaped = projected.reshape(3, count_all, HEADS, HEAD_DIM)
    queries = low(rotate(shaped[0], cosine_tab, sine_tab))
    key_rows = low(rotate(shaped[1], cosine_tab, sine_tab))
    value_rows = low(shaped[2])
    grouped = (queries.reshape(groups, TOK_DEV, HEADS, HEAD_DIM), key_rows.reshape(groups, TOK_DEV, HEADS, HEAD_DIM), value_rows.reshape(groups, TOK_DEV, HEADS, HEAD_DIM), seq_ids.reshape(groups, TOK_DEV))
    attended = lax.map(jax.checkpoint(group_attend), grouped).reshape(count_all, HEADS * HEAD_DIM)
    attended = low(low_back(attended))
    branch_one = low_back(jnp.dot(attended, out_weight, precision=HIGHEST, preferred_element_type=jnp.float32))
    hidden_in = inputs + branch_one
    normed_two = low(layer_norm(hidden_in, gain_two))
    gate_up = low_back(jnp.einsum('td,cdf->ctf', normed_two, gu_weight, precision=HIGHEST))
    activated = low(jax.nn.gelu(gate_up[0], approximate=False) * gate_up[1])
    branch_two = low_back(jnp.dot(activated, down_weight, precision=HIGHEST, preferred_element_type=jnp.float32))
    return hidden_in + branch_two

def reference(tokens, seq_ids, gain_attn, gain_mlp, w_qkv, w_out, w_gu, w_down, cotangent):

    def forward(inputs, gain_one, gain_two, qkv_weight, out_weight, gu_weight, down_weight):
        return layer(inputs, gain_one, gain_two, qkv_weight, out_weight, gu_weight, down_weight, seq_ids)
    output, pullback = jax.vjp(forward, tokens, gain_attn, gain_mlp, w_qkv.astype(jnp.float32), w_out.astype(jnp.float32), w_gu.astype(jnp.float32), w_down.astype(jnp.float32))
    gradients = pullback(cotangent)
    return (output, gradients[0], gradients[1], gradients[2], gradients[3], gradients[4], gradients[5], gradients[6])
```

```python
import functools

import jax
import jax.numpy as jnp
from jax import lax
from jax.experimental import pallas as pl
from jax.experimental.pallas import tpu as pltpu
from jax.sharding import PartitionSpec as P

HEAD_DIM = 64


EPSILON = 1e-05
ROPE_BASE = 160000.0
NEG_FILL = -1e30
INV_ROOT_TWO = 0.7071067811865476
INV_ROOT_TWO_PI = 0.3989422804014327
BLOCK = 256
LAST = (((1,), (1,)), ((), ()))


def norm_rows(values, gain_vec):
    center = values - jnp.mean(values, axis=-1, keepdims=True)
    spread = jnp.mean(center * center, axis=-1, keepdims=True)
    inverse = lax.rsqrt(spread + EPSILON)
    unit_rows = center * inverse
    return (unit_rows * gain_vec, unit_rows, inverse)


def norm_back(grad_rows, unit_rows, inverse, gain_vec):
    scaled = grad_rows * gain_vec
    inner = (
        scaled
        - jnp.mean(scaled, axis=-1, keepdims=True)
        - unit_rows * jnp.mean(scaled * unit_rows, axis=-1, keepdims=True)
    )
    return inner * inverse


def gelu_parts(before_act):
    normal_cdf = 0.5 * (1.0 + lax.erf(before_act * INV_ROOT_TWO))
    density = jnp.exp(-0.5 * before_act * before_act) * INV_ROOT_TWO_PI
    return (before_act * normal_cdf, normal_cdf + before_act * density)


def turn_columns(weights):
    depth, width = weights.shape
    halves = weights.reshape(depth, width // HEAD_DIM, 2, HEAD_DIM // 2)
    return jnp.stack([-halves[:, :, 1], halves[:, :, 0]], axis=2).reshape(depth, width)


def head_rows(rows, head):
    row = lax.broadcasted_iota(jnp.int32, rows.shape, 0)
    inside = (row >= head * HEAD_DIM) & (row < (head + 1) * HEAD_DIM)
    return jnp.where(inside, rows, jnp.zeros_like(rows))


def forward_kernel(
    heads, low_ref, high_ref, idr_ref, idc_ref, q_ref, k_ref, vt_ref, out_ref, log_ref, acc_ref
):
    block = pl.program_id(0)
    ids = idr_ref[...]
    query_t = q_ref[...]
    masked = [head_rows(query_t, head) for head in range(heads)]
    acc_ref[...] = jnp.zeros_like(acc_ref)

    def step(at, carry):
        start = pl.multiple_of(at * BLOCK, BLOCK)
        keys = k_ref[pl.ds(start, BLOCK), :]
        same = idc_ref[pl.ds(start, BLOCK), :] == ids
        result = []
        for head in range(heads):
            top, total = carry[head]
            scores = jnp.dot(keys, masked[head], preferred_element_type=jnp.float32)
            scores = jnp.where(same, scores, NEG_FILL)
            new_top = jnp.maximum(top, jnp.max(scores, axis=0, keepdims=True))
            fade = jnp.exp(top - new_top)
            weights = jnp.exp(scores - new_top)
            total = total * fade + jnp.sum(weights, axis=0, keepdims=True)
            rows = pl.ds(head * HEAD_DIM, HEAD_DIM)
            acc_ref[rows, :] = acc_ref[rows, :] * fade + jnp.dot(
                vt_ref[rows, pl.ds(start, BLOCK)],
                weights.astype(jnp.bfloat16),
                preferred_element_type=jnp.float32,
            )
            result.append((new_top, total))
        return tuple(result)

    first = tuple(
        (jnp.full((1, BLOCK), NEG_FILL, jnp.float32), jnp.zeros((1, BLOCK), jnp.float32))
        for _ in range(heads)
    )
    final = lax.fori_loop(low_ref[block], high_ref[block], step, first)
    for head in range(heads):
        top, total = final[head]
        rows = pl.ds(head * HEAD_DIM, HEAD_DIM)
        out_ref[0, rows, :] = (acc_ref[rows, :] / total).astype(jnp.bfloat16)
        log_ref[head : head + 1, :] = top + jnp.log(total)


def backward_kernel(
    heads,
    low_ref,
    high_ref,
    idr_ref,
    idc_ref,
    q_ref,
    g_ref,
    o_ref,
    log_ref,
    k_ref,
    kt_ref,
    v_ref,
    dq_ref,
    dk_ref,
    dv_ref,
    acc_ref,
):
    block = pl.program_id(0)

    @pl.when(block == 0)
    def _():
        dk_ref[...] = jnp.zeros_like(dk_ref)
        dv_ref[...] = jnp.zeros_like(dv_ref)

    ids = idr_ref[...]
    query_t = q_ref[...]
    grad_t = g_ref[0]
    product = grad_t.astype(jnp.float32) * o_ref[0].astype(jnp.float32)
    masked_q = [head_rows(query_t, head) for head in range(heads)]
    masked_g = [head_rows(grad_t, head) for head in range(heads)]
    inner = [
        jnp.sum(product[head * HEAD_DIM : (head + 1) * HEAD_DIM], axis=0, keepdims=True)
        for head in range(heads)
    ]
    logs = [log_ref[head : head + 1, :] for head in range(heads)]
    acc_ref[...] = jnp.zeros_like(acc_ref)

    def step(at, carry):
        start = pl.multiple_of(at * BLOCK, BLOCK)
        columns = pl.ds(start, BLOCK)
        keys = k_ref[columns, :]
        values = v_ref[columns, :]
        same = idc_ref[columns, :] == ids
        for head in range(heads):
            rows = pl.ds(head * HEAD_DIM, HEAD_DIM)
            scores = jnp.dot(keys, masked_q[head], preferred_element_type=jnp.float32)
            weights = jnp.exp(jnp.where(same, scores - logs[head], NEG_FILL))
            grad_w = jnp.dot(values, masked_g[head], preferred_element_type=jnp.float32)
            grad_s = (weights * (grad_w - inner[head])).astype(jnp.bfloat16)
            dv_ref[rows, columns] += lax.dot_general(
                g_ref[0, rows, :],
                weights.astype(jnp.bfloat16),
                LAST,
                preferred_element_type=jnp.float32,
            )
            dk_ref[rows, columns] += lax.dot_general(
                q_ref[rows, :], grad_s, LAST, preferred_element_type=jnp.float32
            )
            acc_ref[rows, :] += jnp.dot(
                kt_ref[rows, columns], grad_s, preferred_element_type=jnp.float32
            )
        return carry

    lax.fori_loop(low_ref[block], high_ref[block], step, 0)
    dq_ref[...] = acc_ref[...] * (HEAD_DIM**-0.5)


def attend(low, high, id_row, id_column, query_t, keys, value_t, parts):
    width, length = query_t.shape
    heads = width // HEAD_DIM
    per_part = length // parts // BLOCK
    grid_spec = pltpu.PrefetchScalarGridSpec(
        num_scalar_prefetch=2,
        grid=(length // BLOCK,),
        in_specs=[
            pl.BlockSpec((1, BLOCK), lambda i, *_: (0, i)),
            pl.BlockSpec((length, 1), lambda i, *_: (0, 0)),
            pl.BlockSpec((width, BLOCK), lambda i, *_: (0, i)),
            pl.BlockSpec((length, width), lambda i, *_: (0, 0)),
            pl.BlockSpec((width, length), lambda i, *_: (0, 0)),
        ],
        out_specs=[
            pl.BlockSpec((1, width, BLOCK), lambda i, *_: (i // per_part, 0, i % per_part)),
            pl.BlockSpec((heads, BLOCK), lambda i, *_: (0, i)),
        ],
        scratch_shapes=[pltpu.VMEM((width, BLOCK), jnp.float32)],
    )
    return pl.pallas_call(
        functools.partial(forward_kernel, heads),
        grid_spec=grid_spec,
        out_shape=[
            jax.ShapeDtypeStruct((parts, width, length // parts), jnp.bfloat16),
            jax.ShapeDtypeStruct((heads, length), jnp.float32),
        ],
        compiler_params=pltpu.CompilerParams(
            dimension_semantics=("arbitrary",), vmem_limit_bytes=32 * 1024 * 1024
        ),
        cost_estimate=pl.CostEstimate(
            flops=4 * length * length * width,
            bytes_accessed=10 * length * width,
            transcendentals=heads * length * length,
        ),
        name="attend",
    )(low, high, id_row, id_column, query_t, keys, value_t)


def attend_back(
    low, high, id_row, id_column, query_t, grad_t, out_t, logs, keys, key_t, values, parts
):
    width, length = query_t.shape
    heads = width // HEAD_DIM
    per_part = length // parts // BLOCK
    part_spec = pl.BlockSpec((1, width, BLOCK), lambda i, *_: (i // per_part, 0, i % per_part))
    whole_rows = pl.BlockSpec((length, width), lambda i, *_: (0, 0))
    whole_columns = pl.BlockSpec((width, length), lambda i, *_: (0, 0))
    some_columns = pl.BlockSpec((width, BLOCK), lambda i, *_: (0, i))
    grid_spec = pltpu.PrefetchScalarGridSpec(
        num_scalar_prefetch=2,
        grid=(length // BLOCK,),
        in_specs=[
            pl.BlockSpec((1, BLOCK), lambda i, *_: (0, i)),
            pl.BlockSpec((length, 1), lambda i, *_: (0, 0)),
            some_columns,
            part_spec,
            part_spec,
            pl.BlockSpec((heads, BLOCK), lambda i, *_: (0, i)),
            whole_rows,
            whole_columns,
            whole_rows,
        ],
        out_specs=[some_columns, whole_columns, whole_columns],
        scratch_shapes=[pltpu.VMEM((width, BLOCK), jnp.float32)],
    )
    return pl.pallas_call(
        functools.partial(backward_kernel, heads),
        grid_spec=grid_spec,
        out_shape=[jax.ShapeDtypeStruct((width, length), jnp.float32)] * 3,
        compiler_params=pltpu.CompilerParams(
            dimension_semantics=("arbitrary",), vmem_limit_bytes=32 * 1024 * 1024
        ),
        cost_estimate=pl.CostEstimate(
            flops=10 * length * length * width,
            bytes_accessed=24 * length * width,
            transcendentals=heads * length * length,
        ),
        name="attend_back",
    )(low, high, id_row, id_column, query_t, grad_t, out_t, logs, keys, key_t, values)


def turn_back_rows(grad_t, cosine_t, sine_t):
    width, length = grad_t.shape
    half = HEAD_DIM // 2
    split = grad_t.reshape(width // HEAD_DIM, 2, half, length)
    first, second = split[:, 0], split[:, 1]
    return jnp.stack(
        [first * cosine_t + second * sine_t, second * cosine_t - first * sine_t], axis=1
    ).reshape(width, length)


def shards(tokens, seq_ids, gain_attn, gain_mlp, w_qkv, w_out, w_gu, w_down, cotangent):
    f32, bf16 = jnp.float32, jnp.bfloat16
    dot = functools.partial(jnp.einsum, preferred_element_type=f32)
    length = seq_ids.shape[0]
    model = tokens.shape[1]
    width = w_out.shape[0]
    heads = width // HEAD_DIM
    hidden = w_down.shape[0]
    parts = length // tokens.shape[0]
    normed_one, unit_one, inverse_one = norm_rows(tokens, gain_attn)
    normed_all = lax.all_gather(normed_one.astype(bf16), "tensor", axis=0, tiled=True)
    before = jnp.sum((seq_ids[None, :] < seq_ids[:, None]).astype(jnp.int32), axis=1)
    places = (jnp.arange(length, dtype=jnp.int32) - before).astype(f32)
    half = HEAD_DIM // 2
    frequency = ROPE_BASE ** (-(jnp.arange(half, dtype=f32) * 2.0) / HEAD_DIM)
    angles = frequency[:, None] * places[None, :]
    cosine_t, sine_t = jnp.cos(angles), jnp.sin(angles)
    cosine_wide, sine_wide = jnp.tile(cosine_t, (2 * heads, 1)), jnp.tile(sine_t, (2 * heads, 1))
    low = before[::BLOCK] // BLOCK
    last_ids = seq_ids[BLOCK - 1 :: BLOCK]
    upto = jnp.sum((seq_ids[None, :] <= last_ids[:, None]).astype(jnp.int32), axis=1)
    high = (upto + (BLOCK - 1)) // BLOCK
    id_row, id_column = seq_ids[None, :], seq_ids[:, None]
    w_q, w_k, w_v = w_qkv[0], w_qkv[1], w_qkv[2]
    w_all = jnp.concatenate([w_q, w_k, w_v, turn_columns(w_q), turn_columns(w_k)], axis=1)
    projected = dot("de,td->et", w_all, normed_all)
    q_t, k_t, v_t, q_turn, k_turn = [
        projected[i * width : (i + 1) * width] for i in range(5)
    ]
    query_t = ((q_t * cosine_wide + q_turn * sine_wide) * HEAD_DIM**-0.5).astype(bf16)
    key_t = (k_t * cosine_wide + k_turn * sine_wide).astype(bf16)
    value_t = v_t.astype(bf16)
    keys, values = key_t.T, value_t.T
    out_t, logs = attend(low, high, id_row, id_column, query_t, keys, value_t, parts)
    _, s_out, s_gate, s_up, s_down = lax.optimization_barrier(
        (normed_all, w_out, w_gu[0].T, w_gu[1].T, w_down)
    )
    a_out, a_gate, a_up, a_down = [
        lax.all_gather(w, "tensor", axis=0, tiled=True) for w in (s_out, s_gate, s_up, s_down)
    ]
    att_t = lax.all_to_all(out_t, "tensor", 0, 0).reshape(parts * width, tokens.shape[0])
    hidden_in = tokens + dot("et,ed->td", att_t, a_out)
    normed_two, unit_two, inverse_two = norm_rows(hidden_in, gain_mlp)
    normed_two = normed_two.astype(bf16)
    gate = dot("td,fd->tf", normed_two, a_gate)
    up = dot("td,fd->tf", normed_two, a_up)
    gelu_value, gelu_slope = gelu_parts(gate)
    activated = (gelu_value * up).astype(bf16)
    output = hidden_in + dot("tf,fd->td", activated, a_down)
    grad_two = cotangent.astype(bf16)
    grad_act = dot("td,fd->tf", grad_two, a_down)
    grad_gate = (grad_act * up * gelu_slope).astype(bf16)
    grad_up = (grad_act * gelu_value).astype(bf16)
    grad_normed_two = dot("tf,fd->td", grad_gate, a_gate) + dot("tf,fd->td", grad_up, a_up)
    grad_hidden = cotangent + norm_back(grad_normed_two, unit_two, inverse_two, gain_mlp)
    grad_gain_two = jnp.sum(grad_normed_two * unit_two, axis=0)
    grad_one = grad_hidden.astype(bf16)
    grad_att_t = dot("ed,td->et", a_out, grad_one).astype(bf16)
    grad_t = lax.all_to_all(
        grad_att_t.reshape(parts, width, tokens.shape[0]), "tensor", 0, 0
    )
    pieces = [
        dot("tf,td->fd", activated, grad_two).astype(bf16).reshape(parts, hidden, model),
        dot("tf,td->fd", grad_gate, normed_two).astype(bf16).reshape(parts, hidden, model),
        dot("tf,td->fd", grad_up, normed_two).astype(bf16).reshape(parts, hidden, model),
        dot("et,td->ed", att_t, grad_one).astype(bf16).reshape(parts, width, model),
    ]
    stacked = jnp.concatenate(pieces, axis=1)
    stacked, grad_t = lax.optimization_barrier((stacked, grad_t))
    mine = lax.psum_scatter(stacked, "tensor", scatter_dimension=0, tiled=False)
    summed = lax.psum(mine, "dp")
    dq_t, dk_t, dv_t = attend_back(
        low, high, id_row, id_column, query_t, grad_t, out_t, logs, keys, key_t, values, parts
    )
    grad_proj_t = jnp.concatenate(
        [
            turn_back_rows(dq_t, cosine_t, sine_t).astype(bf16),
            turn_back_rows(dk_t, cosine_t, sine_t).astype(bf16),
            dv_t.astype(bf16),
        ],
        axis=0,
    )
    w_flat = jnp.concatenate([w_q, w_k, w_v], axis=1)
    grad_normed_one = lax.psum_scatter(
        dot("et,de->td", grad_proj_t, w_flat).astype(bf16),
        "tensor",
        scatter_dimension=0,
        tiled=True,
    ).astype(f32)
    grad_qkv = dot("td,et->de", normed_all, grad_proj_t)
    grad_gain_one = jnp.sum(grad_qkv * w_flat.astype(f32), axis=1) / gain_attn
    sent, summed = lax.optimization_barrier((grad_qkv.astype(bf16), summed))
    grad_qkv = lax.psum(sent, "dp").astype(f32)
    grad_qkv = jnp.stack([grad_qkv[:, i * width : (i + 1) * width] for i in range(3)])
    gains = lax.psum(jnp.stack([grad_gain_one, grad_gain_two]), ("dp", "tensor"))
    grad_tokens = grad_hidden + norm_back(grad_normed_one, unit_one, inverse_one, gain_attn)
    summed = summed.astype(f32)
    grad_down = summed[:hidden]
    grad_gu = jnp.stack([summed[hidden : 2 * hidden].T, summed[2 * hidden : 3 * hidden].T])
    grad_out = summed[3 * hidden :]
    return (
        output,
        grad_tokens,
        gains[0],
        gains[1],
        grad_qkv,
        grad_out,
        grad_gu,
        grad_down,
    )


def solution(mesh):
    in_specs = (
        P(("dp", "tensor"), None),
        P("dp"),
        P(),
        P(),
        P(None, None, "tensor"),
        P("tensor", None),
        P(None, None, "tensor"),
        P("tensor", None),
        P(("dp", "tensor"), None),
    )
    out_specs = (
        P(("dp", "tensor"), None),
        P(("dp", "tensor"), None),
        P(),
        P(),
        P(None, None, "tensor"),
        P("tensor", None),
        P(None, None, "tensor"),
        P("tensor", None),
    )
    return jax.shard_map(shards, mesh=mesh, in_specs=in_specs, out_specs=out_specs, check_vma=False)
```

```python
import functools

import jax
import jax.numpy as jnp
from jax import lax
from jax.experimental import pallas as pl
from jax.experimental.pallas import tpu as pltpu
from jax.sharding import PartitionSpec as P

HEAD_DIM = 64


EPSILON = 1e-05
ROPE_BASE = 160000.0
NEG_FILL = -1e30
INV_ROOT_TWO = 0.7071067811865476
INV_ROOT_TWO_PI = 0.3989422804014327
BLOCK = 256
LAST = (((1,), (1,)), ((), ()))


def norm_rows(values, gain_vec):
    center = values - jnp.mean(values, axis=-1, keepdims=True)
    spread = jnp.mean(center * center, axis=-1, keepdims=True)
    inverse = lax.rsqrt(spread + EPSILON)
    unit_rows = center * inverse
    return (unit_rows * gain_vec, unit_rows, inverse)


def norm_back(grad_rows, unit_rows, inverse, gain_vec):
    scaled = grad_rows * gain_vec
    inner = (
        scaled
        - jnp.mean(scaled, axis=-1, keepdims=True)
        - unit_rows * jnp.mean(scaled * unit_rows, axis=-1, keepdims=True)
    )
    return inner * inverse


def gelu_parts(before_act):
    normal_cdf = 0.5 * (1.0 + lax.erf(before_act * INV_ROOT_TWO))
    density = jnp.exp(-0.5 * before_act * before_act) * INV_ROOT_TWO_PI
    return (before_act * normal_cdf, normal_cdf + before_act * density)


def turn_columns(weights):
    depth, width = weights.shape
    halves = weights.reshape(depth, width // HEAD_DIM, 2, HEAD_DIM // 2)
    return jnp.stack([-halves[:, :, 1], halves[:, :, 0]], axis=2).reshape(depth, width)


def head_rows(rows, head):
    row = lax.broadcasted_iota(jnp.int32, rows.shape, 0)
    inside = (row >= head * HEAD_DIM) & (row < (head + 1) * HEAD_DIM)
    return jnp.where(inside, rows, jnp.zeros_like(rows))


def forward_kernel(
    heads, low_ref, high_ref, idr_ref, idc_ref, q_ref, k_ref, vt_ref, out_ref, log_ref, acc_ref
):
    block = pl.program_id(0)
    ids = idr_ref[...]
    query_t = q_ref[...]
    masked = [head_rows(query_t, head) for head in range(heads)]
    acc_ref[...] = jnp.zeros_like(acc_ref)

    def step(at, carry):
        start = pl.multiple_of(at * BLOCK, BLOCK)
        keys = k_ref[pl.ds(start, BLOCK), :]
        same = idc_ref[pl.ds(start, BLOCK), :] == ids
        result = []
        for head in range(heads):
            top, total = carry[head]
            scores = jnp.dot(keys, masked[head], preferred_element_type=jnp.float32)
            scores = jnp.where(same, scores, NEG_FILL)
            new_top = jnp.maximum(top, jnp.max(scores, axis=0, keepdims=True))
            fade = jnp.exp(top - new_top)
            weights = jnp.exp(scores - new_top)
            total = total * fade + jnp.sum(weights, axis=0, keepdims=True)
            rows = pl.ds(head * HEAD_DIM, HEAD_DIM)
            acc_ref[rows, :] = acc_ref[rows, :] * fade + jnp.dot(
                vt_ref[rows, pl.ds(start, BLOCK)],
                weights.astype(jnp.bfloat16),
                preferred_element_type=jnp.float32,
            )
            result.append((new_top, total))
        return tuple(result)

    first = tuple(
        (jnp.full((1, BLOCK), NEG_FILL, jnp.float32), jnp.zeros((1, BLOCK), jnp.float32))
        for _ in range(heads)
    )
    final = lax.fori_loop(low_ref[block], high_ref[block], step, first)
    for head in range(heads):
        top, total = final[head]
        rows = pl.ds(head * HEAD_DIM, HEAD_DIM)
        out_ref[0, rows, :] = (acc_ref[rows, :] / total).astype(jnp.bfloat16)
        log_ref[head : head + 1, :] = top + jnp.log(total)


def backward_kernel(
    heads,
    low_ref,
    high_ref,
    idr_ref,
    idc_ref,
    q_ref,
    g_ref,
    o_ref,
    log_ref,
    k_ref,
    kt_ref,
    v_ref,
    dq_ref,
    dk_ref,
    dv_ref,
    acc_ref,
):
    block = pl.program_id(0)

    @pl.when(block == 0)
    def _():
        dk_ref[...] = jnp.zeros_like(dk_ref)
        dv_ref[...] = jnp.zeros_like(dv_ref)

    ids = idr_ref[...]
    query_t = q_ref[...]
    grad_t = g_ref[0]
    product = grad_t.astype(jnp.float32) * o_ref[0].astype(jnp.float32)
    masked_q = [head_rows(query_t, head) for head in range(heads)]
    masked_g = [head_rows(grad_t, head) for head in range(heads)]
    inner = [
        jnp.sum(product[head * HEAD_DIM : (head + 1) * HEAD_DIM], axis=0, keepdims=True)
        for head in range(heads)
    ]
    logs = [log_ref[head : head + 1, :] for head in range(heads)]
    acc_ref[...] = jnp.zeros_like(acc_ref)

    def step(at, carry):
        start = pl.multiple_of(at * BLOCK, BLOCK)
        columns = pl.ds(start, BLOCK)
        keys = k_ref[columns, :]
        values = v_ref[columns, :]
        same = idc_ref[columns, :] == ids
        for head in range(heads):
            rows = pl.ds(head * HEAD_DIM, HEAD_DIM)
            scores = jnp.dot(keys, masked_q[head], preferred_element_type=jnp.float32)
            weights = jnp.exp(jnp.where(same, scores - logs[head], NEG_FILL))
            grad_w = jnp.dot(values, masked_g[head], preferred_element_type=jnp.float32)
            grad_s = (weights * (grad_w - inner[head])).astype(jnp.bfloat16)
            dv_ref[rows, columns] += lax.dot_general(
                g_ref[0, rows, :],
                weights.astype(jnp.bfloat16),
                LAST,
                preferred_element_type=jnp.float32,
            )
            dk_ref[rows, columns] += lax.dot_general(
                q_ref[rows, :], grad_s, LAST, preferred_element_type=jnp.float32
            )
            acc_ref[rows, :] += jnp.dot(
                kt_ref[rows, columns], grad_s, preferred_element_type=jnp.float32
            )
        return carry

    lax.fori_loop(low_ref[block], high_ref[block], step, 0)
    dq_ref[...] = acc_ref[...] * (HEAD_DIM**-0.5)


def attend(low, high, id_row, id_column, query_t, keys, value_t, parts):
    width, length = query_t.shape
    heads = width // HEAD_DIM
    per_part = length // parts // BLOCK
    grid_spec = pltpu.PrefetchScalarGridSpec(
        num_scalar_prefetch=2,
        grid=(length // BLOCK,),
        in_specs=[
            pl.BlockSpec((1, BLOCK), lambda i, *_: (0, i)),
            pl.BlockSpec((length, 1), lambda i, *_: (0, 0)),
            pl.BlockSpec((width, BLOCK), lambda i, *_: (0, i)),
            pl.BlockSpec((length, width), lambda i, *_: (0, 0)),
            pl.BlockSpec((width, length), lambda i, *_: (0, 0)),
        ],
        out_specs=[
            pl.BlockSpec((1, width, BLOCK), lambda i, *_: (i // per_part, 0, i % per_part)),
            pl.BlockSpec((heads, BLOCK), lambda i, *_: (0, i)),
        ],
        scratch_shapes=[pltpu.VMEM((width, BLOCK), jnp.float32)],
    )
    return pl.pallas_call(
        functools.partial(forward_kernel, heads),
        grid_spec=grid_spec,
        out_shape=[
            jax.ShapeDtypeStruct((parts, width, length // parts), jnp.bfloat16),
            jax.ShapeDtypeStruct((heads, length), jnp.float32),
        ],
        compiler_params=pltpu.CompilerParams(
            dimension_semantics=("arbitrary",), vmem_limit_bytes=32 * 1024 * 1024
        ),
        cost_estimate=pl.CostEstimate(
            flops=4 * length * length * width,
            bytes_accessed=10 * length * width,
            transcendentals=heads * length * length,
        ),
        name="attend",
    )(low, high, id_row, id_column, query_t, keys, value_t)


def attend_back(
    low, high, id_row, id_column, query_t, grad_t, out_t, logs, keys, key_t, values, parts
):
    width, length = query_t.shape
    heads = width // HEAD_DIM
    per_part = length // parts // BLOCK
    part_spec = pl.BlockSpec((1, width, BLOCK), lambda i, *_: (i // per_part, 0, i % per_part))
    whole_rows = pl.BlockSpec((length, width), lambda i, *_: (0, 0))
    whole_columns = pl.BlockSpec((width, length), lambda i, *_: (0, 0))
    some_columns = pl.BlockSpec((width, BLOCK), lambda i, *_: (0, i))
    grid_spec = pltpu.PrefetchScalarGridSpec(
        num_scalar_prefetch=2,
        grid=(length // BLOCK,),
        in_specs=[
            pl.BlockSpec((1, BLOCK), lambda i, *_: (0, i)),
            pl.BlockSpec((length, 1), lambda i, *_: (0, 0)),
            some_columns,
            part_spec,
            part_spec,
            pl.BlockSpec((heads, BLOCK), lambda i, *_: (0, i)),
            whole_rows,
            whole_columns,
            whole_rows,
        ],
        out_specs=[some_columns, whole_columns, whole_columns],
        scratch_shapes=[pltpu.VMEM((width, BLOCK), jnp.float32)],
    )
    return pl.pallas_call(
        functools.partial(backward_kernel, heads),
        grid_spec=grid_spec,
        out_shape=[jax.ShapeDtypeStruct((width, length), jnp.float32)] * 3,
        compiler_params=pltpu.CompilerParams(
            dimension_semantics=("arbitrary",), vmem_limit_bytes=32 * 1024 * 1024
        ),
        cost_estimate=pl.CostEstimate(
            flops=10 * length * length * width,
            bytes_accessed=24 * length * width,
            transcendentals=heads * length * length,
        ),
        name="attend_back",
    )(low, high, id_row, id_column, query_t, grad_t, out_t, logs, keys, key_t, values)


def turn_back_rows(grad_t, cosine_t, sine_t):
    width, length = grad_t.shape
    half = HEAD_DIM // 2
    split = grad_t.reshape(width // HEAD_DIM, 2, half, length)
    first, second = split[:, 0], split[:, 1]
    return jnp.stack(
        [first * cosine_t + second * sine_t, second * cosine_t - first * sine_t], axis=1
    ).reshape(width, length)


def swap(values, distance, parts):
    return lax.ppermute(values, "tensor", [(i, i ^ distance) for i in range(parts)])


def sum_groups(values, groups):
    rows, columns = values.shape
    received = lax.all_to_all(values.reshape(groups, rows // groups, columns), "dp", 0, 0)
    share = jnp.sum(received.astype(jnp.float32), axis=0).astype(jnp.bfloat16)
    return lax.all_gather(share, "dp", axis=0, tiled=True)


def shards(tokens, seq_ids, gain_attn, gain_mlp, w_qkv, w_out, w_gu, w_down, cotangent):
    f32, bf16 = jnp.float32, jnp.bfloat16
    dot = functools.partial(jnp.einsum, preferred_element_type=f32)
    length = seq_ids.shape[0]
    model = tokens.shape[1]
    width = w_out.shape[0]
    heads = width // HEAD_DIM
    hidden = w_down.shape[0]
    parts = length // tokens.shape[0]
    normed_one, unit_one, inverse_one = norm_rows(tokens, gain_attn)
    normed_all = lax.all_gather(normed_one.astype(bf16), "tensor", axis=0, tiled=True)
    before = jnp.sum((seq_ids[None, :] < seq_ids[:, None]).astype(jnp.int32), axis=1)
    places = (jnp.arange(length, dtype=jnp.int32) - before).astype(f32)
    half = HEAD_DIM // 2
    frequency = ROPE_BASE ** (-(jnp.arange(half, dtype=f32) * 2.0) / HEAD_DIM)
    angles = frequency[:, None] * places[None, :]
    cosine_t, sine_t = jnp.cos(angles), jnp.sin(angles)
    cosine_wide, sine_wide = jnp.tile(cosine_t, (2 * heads, 1)), jnp.tile(sine_t, (2 * heads, 1))
    low = before[::BLOCK] // BLOCK
    last_ids = seq_ids[BLOCK - 1 :: BLOCK]
    upto = jnp.sum((seq_ids[None, :] <= last_ids[:, None]).astype(jnp.int32), axis=1)
    high = (upto + (BLOCK - 1)) // BLOCK
    id_row, id_column = seq_ids[None, :], seq_ids[:, None]
    w_q, w_k, w_v = w_qkv[0], w_qkv[1], w_qkv[2]
    w_all = jnp.concatenate([w_q, w_k, w_v, turn_columns(w_q), turn_columns(w_k)], axis=1)
    projected = dot("de,td->et", w_all, normed_all)
    q_t, k_t, v_t, q_turn, k_turn = [
        projected[i * width : (i + 1) * width] for i in range(5)
    ]
    query_t = ((q_t * cosine_wide + q_turn * sine_wide) * HEAD_DIM**-0.5).astype(bf16)
    key_t = (k_t * cosine_wide + k_turn * sine_wide).astype(bf16)
    value_t = v_t.astype(bf16)
    keys, values = key_t.T, value_t.T
    out_t, logs = attend(low, high, id_row, id_column, query_t, keys, value_t, parts)
    _, s_out, s_gate, s_up, s_down = lax.optimization_barrier(
        (normed_all, w_out, w_gu[0].T, w_gu[1].T, w_down)
    )
    a_out = lax.all_gather(s_out, "tensor", axis=0, tiled=True)
    shards_own = (s_gate, s_up, s_down)
    shards_across = [swap(w, 2, parts) for w in shards_own]
    out_t, *shards_across = lax.optimization_barrier((out_t, *shards_across))
    a_gate, a_up, a_down = [
        jnp.concatenate([own, across, swap(own, 1, parts), swap(across, 1, parts)], axis=0)
        for own, across in zip(shards_own, shards_across)
    ]
    att_t = lax.all_to_all(out_t, "tensor", 0, 0).reshape(parts * width, tokens.shape[0])
    hidden_in = tokens + dot("et,ed->td", att_t, a_out)
    normed_two, unit_two, inverse_two = norm_rows(hidden_in, gain_mlp)
    normed_two = normed_two.astype(bf16)
    gate = dot("td,fd->tf", normed_two, a_gate)
    up = dot("td,fd->tf", normed_two, a_up)
    gelu_value, gelu_slope = gelu_parts(gate)
    activated = (gelu_value * up).astype(bf16)
    output = hidden_in + dot("tf,fd->td", activated, a_down)
    grad_two = cotangent.astype(bf16)
    grad_act = dot("td,fd->tf", grad_two, a_down)
    grad_gate = (grad_act * up * gelu_slope).astype(bf16)
    grad_up = (grad_act * gelu_value).astype(bf16)
    grad_normed_two = dot("tf,fd->td", grad_gate, a_gate) + dot("tf,fd->td", grad_up, a_up)
    grad_hidden = cotangent + norm_back(grad_normed_two, unit_two, inverse_two, gain_mlp)
    grad_gain_two = jnp.sum(grad_normed_two * unit_two, axis=0)
    grad_one = grad_hidden.astype(bf16)
    grad_att_t = dot("ed,td->et", a_out, grad_one).astype(bf16)
    grad_t = lax.all_to_all(
        grad_att_t.reshape(parts, width, tokens.shape[0]), "tensor", 0, 0
    )
    grads_mlp = jnp.stack(
        [
            dot("tf,td->fd", activated, grad_two).astype(bf16).reshape(parts, hidden, model),
            dot("tf,td->fd", grad_gate, normed_two).astype(bf16).reshape(parts, hidden, model),
            dot("tf,td->fd", grad_up, normed_two).astype(bf16).reshape(parts, hidden, model),
        ],
        axis=1,
    )
    half_mlp = (grads_mlp[:2].astype(f32) + swap(grads_mlp[2:], 1, parts).astype(f32)).astype(bf16)
    grads_out = dot("et,td->ed", att_t, grad_one).astype(bf16).reshape(parts, width, model)
    gain_rows = jnp.broadcast_to(grad_gain_two.astype(bf16), (parts, 16, model))
    grads_out = jnp.concatenate([grads_out, gain_rows], axis=1)
    half_mlp, grads_out, grad_t = lax.optimization_barrier((half_mlp, grads_out, grad_t))
    mlp_mine = (half_mlp[0].astype(f32) + swap(half_mlp[1], 2, parts).astype(f32)).astype(bf16)
    out_mine = lax.psum_scatter(grads_out, "tensor", scatter_dimension=0, tiled=False)
    dq_t, dk_t, dv_t = attend_back(
        low, high, id_row, id_column, query_t, grad_t, out_t, logs, keys, key_t, values, parts
    )
    dq_t, dk_t, dv_t, mlp_mine = lax.optimization_barrier((dq_t, dk_t, dv_t, mlp_mine))
    grad_proj_t = jnp.concatenate(
        [
            turn_back_rows(dq_t, cosine_t, sine_t).astype(bf16),
            turn_back_rows(dk_t, cosine_t, sine_t).astype(bf16),
            dv_t.astype(bf16),
        ],
        axis=0,
    )
    w_flat = jnp.concatenate([w_q, w_k, w_v], axis=1)
    product = dot("et,de->td", grad_proj_t, w_flat).astype(bf16).reshape(parts, -1, model)
    me = lax.axis_index("tensor")
    mine_two, across_two, other_two, cross_two = [
        lax.dynamic_index_in_dim(product, me ^ bits, 0, keepdims=False).astype(f32)
        for bits in (0, 2, 1, 3)
    ]
    across_two = (across_two + swap(cross_two.astype(bf16), 1, parts).astype(f32)).astype(bf16)
    mine_two = mine_two + swap(other_two.astype(bf16), 1, parts).astype(f32)
    grad_normed_one = mine_two + swap(across_two, 2, parts).astype(f32)
    grad_qkv = dot("td,et->de", normed_all, grad_proj_t)
    groups = lax.axis_size("dp")
    grad_qkv = sum_groups(grad_qkv.astype(bf16), groups).astype(f32)
    count = 3 * hidden + width + 16
    padding = -count % (16 * groups)
    mine = jnp.concatenate(
        [mlp_mine.reshape(3 * hidden, model), out_mine, jnp.zeros((padding, model), bf16)]
    )
    summed = sum_groups(mine, groups)
    gain_one = lax.psum(jnp.sum(grad_qkv * w_flat.astype(f32), axis=1) / gain_attn, "tensor")
    grad_qkv = jnp.stack([grad_qkv[:, i * width : (i + 1) * width] for i in range(3)])
    grad_tokens = grad_hidden + norm_back(grad_normed_one, unit_one, inverse_one, gain_attn)
    summed = summed.astype(f32)
    grad_down = summed[:hidden]
    grad_gu = jnp.stack([summed[hidden : 2 * hidden].T, summed[2 * hidden : 3 * hidden].T])
    grad_out = summed[3 * hidden : 3 * hidden + width]
    gain_two = summed[3 * hidden + width]
    return (
        output,
        grad_tokens,
        gain_one,
        gain_two,
        grad_qkv,
        grad_out,
        grad_gu,
        grad_down,
    )


def solution(mesh):
    in_specs = (
        P(("dp", "tensor"), None),
        P("dp"),
        P(),
        P(),
        P(None, None, "tensor"),
        P("tensor", None),
        P(None, None, "tensor"),
        P("tensor", None),
        P(("dp", "tensor"), None),
    )
    out_specs = (
        P(("dp", "tensor"), None),
        P(("dp", "tensor"), None),
        P(),
        P(),
        P(None, None, "tensor"),
        P("tensor", None),
        P(None, None, "tensor"),
        P("tensor", None),
    )
    return jax.shard_map(shards, mesh=mesh, in_specs=in_specs, out_specs=out_specs, check_vma=False)
```

```python
import functools

import jax
import jax.numpy as jnp
from jax import lax
from jax.experimental import pallas as pl
from jax.experimental.pallas import tpu as pltpu
from jax.sharding import PartitionSpec as P

HEAD_DIM = 64


EPSILON = 1e-05
ROPE_BASE = 160000.0
NEG_FILL = -1e30
INV_ROOT_TWO = 0.7071067811865476
INV_ROOT_TWO_PI = 0.3989422804014327
BLOCK = 256
LAST = (((1,), (1,)), ((), ()))


def norm_rows(values, gain_vec):
    center = values - jnp.mean(values, axis=-1, keepdims=True)
    spread = jnp.mean(center * center, axis=-1, keepdims=True)
    inverse = lax.rsqrt(spread + EPSILON)
    unit_rows = center * inverse
    return (unit_rows * gain_vec, unit_rows, inverse)


def norm_back(grad_rows, unit_rows, inverse, gain_vec):
    scaled = grad_rows * gain_vec
    inner = (
        scaled
        - jnp.mean(scaled, axis=-1, keepdims=True)
        - unit_rows * jnp.mean(scaled * unit_rows, axis=-1, keepdims=True)
    )
    return inner * inverse


def gelu_parts(before_act):
    normal_cdf = 0.5 * (1.0 + lax.erf(before_act * INV_ROOT_TWO))
    density = jnp.exp(-0.5 * before_act * before_act) * INV_ROOT_TWO_PI
    return (before_act * normal_cdf, normal_cdf + before_act * density)


def turn_columns(weights):
    depth, width = weights.shape
    halves = weights.reshape(depth, width // HEAD_DIM, 2, HEAD_DIM // 2)
    return jnp.stack([-halves[:, :, 1], halves[:, :, 0]], axis=2).reshape(depth, width)


def head_rows(rows, head):
    row = lax.broadcasted_iota(jnp.int32, rows.shape, 0)
    inside = (row >= head * HEAD_DIM) & (row < (head + 1) * HEAD_DIM)
    return jnp.where(inside, rows, jnp.zeros_like(rows))


def forward_kernel(
    heads, low_ref, high_ref, idr_ref, idc_ref, q_ref, k_ref, vt_ref, out_ref, log_ref, acc_ref
):
    block = pl.program_id(0)
    ids = idr_ref[...]
    query_t = q_ref[...]
    masked = [head_rows(query_t, head) for head in range(heads)]
    acc_ref[...] = jnp.zeros_like(acc_ref)

    def step(at, carry):
        start = pl.multiple_of(at * BLOCK, BLOCK)
        keys = k_ref[pl.ds(start, BLOCK), :]
        same = idc_ref[pl.ds(start, BLOCK), :] == ids
        result = []
        for head in range(heads):
            top, total = carry[head]
            scores = jnp.dot(keys, masked[head], preferred_element_type=jnp.float32)
            scores = jnp.where(same, scores, NEG_FILL)
            new_top = jnp.maximum(top, jnp.max(scores, axis=0, keepdims=True))
            fade = jnp.exp(top - new_top)
            weights = jnp.exp(scores - new_top)
            total = total * fade + jnp.sum(weights, axis=0, keepdims=True)
            rows = pl.ds(head * HEAD_DIM, HEAD_DIM)
            acc_ref[rows, :] = acc_ref[rows, :] * fade + jnp.dot(
                vt_ref[rows, pl.ds(start, BLOCK)],
                weights.astype(jnp.bfloat16),
                preferred_element_type=jnp.float32,
            )
            result.append((new_top, total))
        return tuple(result)

    first = tuple(
        (jnp.full((1, BLOCK), NEG_FILL, jnp.float32), jnp.zeros((1, BLOCK), jnp.float32))
        for _ in range(heads)
    )
    final = lax.fori_loop(low_ref[block], high_ref[block], step, first)
    for head in range(heads):
        top, total = final[head]
        rows = pl.ds(head * HEAD_DIM, HEAD_DIM)
        out_ref[0, rows, :] = (acc_ref[rows, :] / total).astype(jnp.bfloat16)
        log_ref[head : head + 1, :] = top + jnp.log(total)


def backward_kernel(
    heads,
    low_ref,
    high_ref,
    idr_ref,
    idc_ref,
    q_ref,
    g_ref,
    o_ref,
    log_ref,
    k_ref,
    kt_ref,
    v_ref,
    dq_ref,
    dk_ref,
    dv_ref,
    acc_ref,
):
    block = pl.program_id(0)

    @pl.when(block == 0)
    def _():
        dk_ref[...] = jnp.zeros_like(dk_ref)
        dv_ref[...] = jnp.zeros_like(dv_ref)

    ids = idr_ref[...]
    query_t = q_ref[...]
    grad_t = g_ref[0]
    product = grad_t.astype(jnp.float32) * o_ref[0].astype(jnp.float32)
    masked_q = [head_rows(query_t, head) for head in range(heads)]
    masked_g = [head_rows(grad_t, head) for head in range(heads)]
    inner = [
        jnp.sum(product[head * HEAD_DIM : (head + 1) * HEAD_DIM], axis=0, keepdims=True)
        for head in range(heads)
    ]
    logs = [log_ref[head : head + 1, :] for head in range(heads)]
    acc_ref[...] = jnp.zeros_like(acc_ref)

    def step(at, carry):
        start = pl.multiple_of(at * BLOCK, BLOCK)
        columns = pl.ds(start, BLOCK)
        keys = k_ref[columns, :]
        values = v_ref[columns, :]
        same = idc_ref[columns, :] == ids
        for head in range(heads):
            rows = pl.ds(head * HEAD_DIM, HEAD_DIM)
            scores = jnp.dot(keys, masked_q[head], preferred_element_type=jnp.float32)
            weights = jnp.exp(jnp.where(same, scores - logs[head], NEG_FILL))
            grad_w = jnp.dot(values, masked_g[head], preferred_element_type=jnp.float32)
            grad_s = (weights * (grad_w - inner[head])).astype(jnp.bfloat16)
            dv_ref[rows, columns] += lax.dot_general(
                g_ref[0, rows, :],
                weights.astype(jnp.bfloat16),
                LAST,
                preferred_element_type=jnp.float32,
            )
            dk_ref[rows, columns] += lax.dot_general(
                q_ref[rows, :], grad_s, LAST, preferred_element_type=jnp.float32
            )
            acc_ref[rows, :] += jnp.dot(
                kt_ref[rows, columns], grad_s, preferred_element_type=jnp.float32
            )
        return carry

    lax.fori_loop(low_ref[block], high_ref[block], step, 0)
    dq_ref[...] = acc_ref[...] * (HEAD_DIM**-0.5)


def attend(low, high, id_row, id_column, query_t, keys, value_t, parts):
    width, length = query_t.shape
    heads = width // HEAD_DIM
    per_part = length // parts // BLOCK
    grid_spec = pltpu.PrefetchScalarGridSpec(
        num_scalar_prefetch=2,
        grid=(length // BLOCK,),
        in_specs=[
            pl.BlockSpec((1, BLOCK), lambda i, *_: (0, i)),
            pl.BlockSpec((length, 1), lambda i, *_: (0, 0)),
            pl.BlockSpec((width, BLOCK), lambda i, *_: (0, i)),
            pl.BlockSpec((length, width), lambda i, *_: (0, 0)),
            pl.BlockSpec((width, length), lambda i, *_: (0, 0)),
        ],
        out_specs=[
            pl.BlockSpec((1, width, BLOCK), lambda i, *_: (i // per_part, 0, i % per_part)),
            pl.BlockSpec((heads, BLOCK), lambda i, *_: (0, i)),
        ],
        scratch_shapes=[pltpu.VMEM((width, BLOCK), jnp.float32)],
    )
    return pl.pallas_call(
        functools.partial(forward_kernel, heads),
        grid_spec=grid_spec,
        out_shape=[
            jax.ShapeDtypeStruct((parts, width, length // parts), jnp.bfloat16),
            jax.ShapeDtypeStruct((heads, length), jnp.float32),
        ],
        compiler_params=pltpu.CompilerParams(
            dimension_semantics=("arbitrary",), vmem_limit_bytes=32 * 1024 * 1024
        ),
        cost_estimate=pl.CostEstimate(
            flops=4 * length * length * width,
            bytes_accessed=10 * length * width,
            transcendentals=heads * length * length,
        ),
        name="attend",
    )(low, high, id_row, id_column, query_t, keys, value_t)


def attend_back(
    low, high, id_row, id_column, query_t, grad_t, out_t, logs, keys, key_t, values, parts
):
    width, length = query_t.shape
    heads = width // HEAD_DIM
    per_part = length // parts // BLOCK
    part_spec = pl.BlockSpec((1, width, BLOCK), lambda i, *_: (i // per_part, 0, i % per_part))
    whole_rows = pl.BlockSpec((length, width), lambda i, *_: (0, 0))
    whole_columns = pl.BlockSpec((width, length), lambda i, *_: (0, 0))
    some_columns = pl.BlockSpec((width, BLOCK), lambda i, *_: (0, i))
    grid_spec = pltpu.PrefetchScalarGridSpec(
        num_scalar_prefetch=2,
        grid=(length // BLOCK,),
        in_specs=[
            pl.BlockSpec((1, BLOCK), lambda i, *_: (0, i)),
            pl.BlockSpec((length, 1), lambda i, *_: (0, 0)),
            some_columns,
            part_spec,
            part_spec,
            pl.BlockSpec((heads, BLOCK), lambda i, *_: (0, i)),
            whole_rows,
            whole_columns,
            whole_rows,
        ],
        out_specs=[some_columns, whole_columns, whole_columns],
        scratch_shapes=[pltpu.VMEM((width, BLOCK), jnp.float32)],
    )
    return pl.pallas_call(
        functools.partial(backward_kernel, heads),
        grid_spec=grid_spec,
        out_shape=[jax.ShapeDtypeStruct((width, length), jnp.float32)] * 3,
        compiler_params=pltpu.CompilerParams(
            dimension_semantics=("arbitrary",), vmem_limit_bytes=32 * 1024 * 1024
        ),
        cost_estimate=pl.CostEstimate(
            flops=10 * length * length * width,
            bytes_accessed=24 * length * width,
            transcendentals=heads * length * length,
        ),
        name="attend_back",
    )(low, high, id_row, id_column, query_t, grad_t, out_t, logs, keys, key_t, values)


def turn_back_rows(grad_t, cosine_t, sine_t):
    width, length = grad_t.shape
    half = HEAD_DIM // 2
    split = grad_t.reshape(width // HEAD_DIM, 2, half, length)
    first, second = split[:, 0], split[:, 1]
    return jnp.stack(
        [first * cosine_t + second * sine_t, second * cosine_t - first * sine_t], axis=1
    ).reshape(width, length)


def swap(values, distance, parts):
    return lax.ppermute(values, "tensor", [(i, i ^ distance) for i in range(parts)])


def share_of(values, groups):
    rows, columns = values.shape
    received = lax.all_to_all(values.reshape(groups, rows // groups, columns), "dp", 0, 0)
    return jnp.sum(received.astype(jnp.float32), axis=0).astype(jnp.bfloat16)


def sum_groups(values, groups):
    return lax.all_gather(share_of(values, groups), "dp", axis=0, tiled=True)


def shards(tokens, seq_ids, gain_attn, gain_mlp, w_qkv, w_out, w_gu, w_down, cotangent):
    f32, bf16 = jnp.float32, jnp.bfloat16
    dot = functools.partial(jnp.einsum, preferred_element_type=f32)
    length = seq_ids.shape[0]
    model = tokens.shape[1]
    width = w_out.shape[0]
    heads = width // HEAD_DIM
    hidden = w_down.shape[0]
    parts = length // tokens.shape[0]
    normed_one, unit_one, inverse_one = norm_rows(tokens, gain_attn)
    normed_all = lax.all_gather(normed_one.astype(bf16), "tensor", axis=0, tiled=True)
    before = jnp.sum((seq_ids[None, :] < seq_ids[:, None]).astype(jnp.int32), axis=1)
    places = (jnp.arange(length, dtype=jnp.int32) - before).astype(f32)
    half = HEAD_DIM // 2
    frequency = ROPE_BASE ** (-(jnp.arange(half, dtype=f32) * 2.0) / HEAD_DIM)
    angles = frequency[:, None] * places[None, :]
    cosine_t, sine_t = jnp.cos(angles), jnp.sin(angles)
    cosine_wide, sine_wide = jnp.tile(cosine_t, (2 * heads, 1)), jnp.tile(sine_t, (2 * heads, 1))
    low = before[::BLOCK] // BLOCK
    last_ids = seq_ids[BLOCK - 1 :: BLOCK]
    upto = jnp.sum((seq_ids[None, :] <= last_ids[:, None]).astype(jnp.int32), axis=1)
    high = (upto + (BLOCK - 1)) // BLOCK
    id_row, id_column = seq_ids[None, :], seq_ids[:, None]
    w_q, w_k, w_v = w_qkv[0], w_qkv[1], w_qkv[2]
    w_all = jnp.concatenate([w_q, w_k, w_v, turn_columns(w_q), turn_columns(w_k)], axis=1)
    projected = dot("de,td->et", w_all, normed_all)
    q_t, k_t, v_t, q_turn, k_turn = [
        projected[i * width : (i + 1) * width] for i in range(5)
    ]
    query_t = ((q_t * cosine_wide + q_turn * sine_wide) * HEAD_DIM**-0.5).astype(bf16)
    key_t = (k_t * cosine_wide + k_turn * sine_wide).astype(bf16)
    value_t = v_t.astype(bf16)
    keys, values = key_t.T, value_t.T
    out_t, logs = attend(low, high, id_row, id_column, query_t, keys, value_t, parts)
    _, s_out, s_gate, s_up, s_down = lax.optimization_barrier(
        (normed_all, w_out, w_gu[0].T, w_gu[1].T, w_down)
    )
    a_out = lax.all_gather(s_out, "tensor", axis=0, tiled=True)
    shards_own = (s_gate, s_up, s_down)
    shards_across = [swap(w, 2, parts) for w in shards_own]
    out_t, *shards_across = lax.optimization_barrier((out_t, *shards_across))
    a_gate, a_up, a_down = [
        jnp.concatenate([own, across, swap(own, 1, parts), swap(across, 1, parts)], axis=0)
        for own, across in zip(shards_own, shards_across)
    ]
    att_t = lax.all_to_all(out_t, "tensor", 0, 0).reshape(parts * width, tokens.shape[0])
    hidden_in = tokens + dot("et,ed->td", att_t, a_out)
    normed_two, unit_two, inverse_two = norm_rows(hidden_in, gain_mlp)
    normed_two = normed_two.astype(bf16)
    gate = dot("td,fd->tf", normed_two, a_gate)
    up = dot("td,fd->tf", normed_two, a_up)
    gelu_value, gelu_slope = gelu_parts(gate)
    activated = (gelu_value * up).astype(bf16)
    output = hidden_in + dot("tf,fd->td", activated, a_down)
    grad_two = cotangent.astype(bf16)
    grad_act = dot("td,fd->tf", grad_two, a_down)
    grad_gate = (grad_act * up * gelu_slope).astype(bf16)
    grad_up = (grad_act * gelu_value).astype(bf16)
    grad_normed_two = dot("tf,fd->td", grad_gate, a_gate) + dot("tf,fd->td", grad_up, a_up)
    grad_hidden = cotangent + norm_back(grad_normed_two, unit_two, inverse_two, gain_mlp)
    grad_gain_two = jnp.sum(grad_normed_two * unit_two, axis=0)
    grad_one = grad_hidden.astype(bf16)
    grad_att_t = dot("ed,td->et", a_out, grad_one).astype(bf16)
    grad_t = lax.all_to_all(
        grad_att_t.reshape(parts, width, tokens.shape[0]), "tensor", 0, 0
    )
    grads_mlp = jnp.stack(
        [
            dot("tf,td->fd", activated, grad_two).astype(bf16).reshape(parts, hidden, model),
            dot("tf,td->fd", grad_gate, normed_two).astype(bf16).reshape(parts, hidden, model),
            dot("tf,td->fd", grad_up, normed_two).astype(bf16).reshape(parts, hidden, model),
        ],
        axis=1,
    )
    half_mlp = (grads_mlp[:2].astype(f32) + swap(grads_mlp[2:], 1, parts).astype(f32)).astype(bf16)
    grads_out = dot("et,td->ed", att_t, grad_one).astype(bf16).reshape(parts, width, model)
    gain_rows = jnp.broadcast_to(grad_gain_two.astype(bf16), (parts, 16, model))
    grads_out = jnp.concatenate([grads_out, gain_rows], axis=1)
    half_mlp, grads_out, grad_t = lax.optimization_barrier((half_mlp, grads_out, grad_t))
    mlp_mine = (half_mlp[0].astype(f32) + swap(half_mlp[1], 2, parts).astype(f32)).astype(bf16)
    out_mine = lax.psum_scatter(grads_out, "tensor", scatter_dimension=0, tiled=False)
    dq_t, dk_t, dv_t = attend_back(
        low, high, id_row, id_column, query_t, grad_t, out_t, logs, keys, key_t, values, parts
    )
    dq_t, dk_t, dv_t, mlp_mine = lax.optimization_barrier((dq_t, dk_t, dv_t, mlp_mine))
    grad_proj_t = jnp.concatenate(
        [
            turn_back_rows(dq_t, cosine_t, sine_t).astype(bf16),
            turn_back_rows(dk_t, cosine_t, sine_t).astype(bf16),
            dv_t.astype(bf16),
        ],
        axis=0,
    )
    w_flat = jnp.concatenate([w_q, w_k, w_v], axis=1)
    product = dot("et,de->td", grad_proj_t, w_flat).astype(bf16).reshape(parts, -1, model)
    me = lax.axis_index("tensor")
    mine_two, across_two, other_two, cross_two = [
        lax.dynamic_index_in_dim(product, me ^ bits, 0, keepdims=False).astype(f32)
        for bits in (0, 2, 1, 3)
    ]
    across_two = (across_two + swap(cross_two.astype(bf16), 1, parts).astype(f32)).astype(bf16)
    mine_two = mine_two + swap(other_two.astype(bf16), 1, parts).astype(f32)
    grad_normed_one = mine_two + swap(across_two, 2, parts).astype(f32)
    grad_qkv = dot("td,et->de", normed_all, grad_proj_t)
    groups = lax.axis_size("dp")
    qkv_share = share_of(grad_qkv.astype(bf16), groups)
    count = 3 * hidden + width + 16
    padding = -count % (16 * groups)
    mine = jnp.concatenate(
        [mlp_mine.reshape(3 * hidden, model), out_mine, jnp.zeros((padding, model), bf16)]
    )
    mine, qkv_share = lax.optimization_barrier((mine, qkv_share))
    grad_qkv = lax.all_gather(qkv_share, "dp", axis=0, tiled=True).astype(f32)
    summed = sum_groups(mine, groups)
    gain_one = lax.psum(jnp.sum(grad_qkv * w_flat.astype(f32), axis=1) / gain_attn, "tensor")
    grad_qkv = jnp.stack([grad_qkv[:, i * width : (i + 1) * width] for i in range(3)])
    grad_tokens = grad_hidden + norm_back(grad_normed_one, unit_one, inverse_one, gain_attn)
    summed = summed.astype(f32)
    grad_down = summed[:hidden]
    grad_gu = jnp.stack([summed[hidden : 2 * hidden].T, summed[2 * hidden : 3 * hidden].T])
    grad_out = summed[3 * hidden : 3 * hidden + width]
    gain_two = summed[3 * hidden + width]
    return (
        output,
        grad_tokens,
        gain_one,
        gain_two,
        grad_qkv,
        grad_out,
        grad_gu,
        grad_down,
    )


def solution(mesh):
    in_specs = (
        P(("dp", "tensor"), None),
        P("dp"),
        P(),
        P(),
        P(None, None, "tensor"),
        P("tensor", None),
        P(None, None, "tensor"),
        P("tensor", None),
        P(("dp", "tensor"), None),
    )
    out_specs = (
        P(("dp", "tensor"), None),
        P(("dp", "tensor"), None),
        P(),
        P(),
        P(None, None, "tensor"),
        P("tensor", None),
        P(None, None, "tensor"),
        P("tensor", None),
    )
    return jax.shard_map(shards, mesh=mesh, in_specs=in_specs, out_specs=out_specs, check_vma=False)
```
